32 devices in a mesh: groups: 2 (over y), lat: 4 (over z), dm: 2 (over x), sub: 2 (over core).
Axes of the slice: x: 2, y: 2, z: 4, core: 2. Of those that a mesh axis runs over, the one named last changes fastest.
Arguments:
- tokens: bfloat16 [1024, 3584], P(('groups', 'lat'), 'dm'), parts along dimension 0, may hold values from -6 to 6
- cotangent: bfloat16 [1024, 3584], P(('groups', 'lat'), 'dm'), parts along dimension 0, may hold values from -6 to 6
- enc_weight: bfloat16 [3584, 8192], P('dm', ('lat', 'sub')), may hold values from -0.09375 to 0.09375
- enc_bias: float32 [8192], P(('lat', 'sub')), may hold values from -3 to 3
- threshold: float32 [8192], P(('lat', 'sub')), may hold values from 0.05 to 1.5
- dec_weight: bfloat16 [8192, 3584], P(('lat', 'sub'), 'dm'), may hold values from -0.0625 to 0.0625
- dec_bias: float32 [3584], P('dm'), may hold values from -3 to 3
- blocks: int32 [8, 8, 12], P('groups', ('lat', 'sub')), parts along dimension 0, may hold values from 0 to 127, as said below
- counts: int32 [8, 8], P('groups', ('lat', 'sub')), parts along dimension 0, may hold values from 0 to 12, as said below
Outputs:
- reconstruction: bfloat16 [1024, 3584], P(('groups', 'lat'), 'dm'), parts along dimension 0
- input_grad: bfloat16 [1024, 3584], P(('groups', 'lat'), 'dm'), parts along dimension 0
- attribution: float32 [16384], P(('groups', 'lat', 'sub')), parts along dimension 0
The draws below stay inside these ranges and needn't reach their ends.
There are 2 independent parts, one for each index of `groups`. The reference program is written for one: setup_inputs(seed, part) draws one part's arguments, and reference() takes and returns one part's arrays. A program takes and returns all parts, laid end to end along the dimension named above; an argument that names none is the same for every part. Nothing has to cross between parts.
Inputs may be any that keep to these rules, and one draw needn't show every extreme that they name: blocks[t, h, k] is a block of shard h, h * 16 <= blocks[t, h, k] < (h + 1) * 16; the 12 slots of one tile and shard name different blocks. `counts`: in every draw some shard has all 12 slots live in every tile.
All inputs are finite; a program needn't handle non-finite values.
Results may differ from the reference program's by a relative error of at most 0.0049.
Values may be sent and summed in bfloat16 or wider, within the bound.
A program may use at most 128 MiB of HBM per device.

```python
import math
import jax
import jax.numpy as jnp
from jax import lax

D = 3584
BLK = 64
BLK_DEV = 16
BPU = 12
TILE = 128
TILES = 4
F = 8192
TOKENS = 512
N_LAT = 4
N_SUB = 2


def draw_blocks(key, part):
    key = jax.random.fold_in(key, 11)
    shard_count = N_LAT * N_SUB
    shape = (TILES, shard_count, BLK_DEV)
    scores = jax.random.randint(key, shape, 0, 4096) * BLK_DEV + lax.broadcasted_iota(jnp.int32, shape, 2)
    order = jnp.argsort(scores, axis=2)[:, :, :BPU]
    base = lax.broadcasted_iota(jnp.int32, (TILES, shard_count, BPU), 1) * BLK_DEV
    return (base + order).astype(jnp.int32)


def draw_counts(key, part):
    key = jax.random.fold_in(key, 23)
    heat_key, count_key, hot_key = jax.random.split(key, 3)
    shard_count = N_LAT * N_SUB
    heat = jax.random.randint(heat_key, (1, shard_count), 0, BPU + 1)
    raw = jax.random.randint(count_key, (TILES, shard_count), 0, BPU + 1)
    hot = jax.random.randint(hot_key, (), 0, shard_count)
    is_hot = lax.broadcasted_iota(jnp.int32, (TILES, shard_count), 1) == hot
    return jnp.where(is_hot, BPU, jnp.minimum(raw, heat)).astype(jnp.int32)


def block_levels(rng, extent, pieces, low, largest):
    level = 1.0
    for dim, blocks in pieces:
        steps = jax.random.uniform(jax.random.fold_in(jax.random.fold_in(rng, 6), dim), (blocks,), jnp.float32, low / len(pieces), largest / len(pieces))
        level = level * jnp.repeat(jnp.exp(steps), extent[dim] // blocks).reshape((-1,) + (1,) * (len(extent) - 1 - dim))
    return level


def scatter_about(rng, extent, width, most, pieces=(), kind=jnp.bfloat16):
    loudness = block_levels(rng, extent, pieces, -0.22, 0.18) if pieces else 1.0
    drawn = jax.random.normal(rng, extent, jnp.float32) * width * loudness
    return jnp.minimum(jnp.maximum(drawn, -most), most).astype(kind)


def setup_inputs(seed: int = 0, part: int = 0) -> dict:
    arg_keys = jax.random.split(jax.random.key(seed), 10)
    own_keys = jax.random.split(jax.random.fold_in(arg_keys[9], part), 10)
    return {
        "tokens": scatter_about(own_keys[0], (TOKENS, D), 1.0, 6.0, ((0, 4), (1, 2))),
        "cotangent": scatter_about(own_keys[1], (TOKENS, D), 1.0, 6.0, ((0, 4), (1, 2))),
        "enc_weight": scatter_about(arg_keys[2], (D, F), D ** -0.5, 0.09375, ((0, 2), (1, 8))),
        "enc_bias": scatter_about(arg_keys[3], (F,), 0.5, 3.0, ((0, 8),), jnp.float32),
        "threshold": jnp.clip(jnp.exp(math.log(1.5) - 3.4011974 * jax.random.uniform(arg_keys[4], (F,), jnp.float32) ** block_levels(arg_keys[4], (F,), ((0, 8),), -0.2, 0.2)), 0.05, 1.5),
        "dec_weight": scatter_about(arg_keys[5], (F, D), F ** -0.5, 0.0625, ((0, 8), (1, 2))),
        "dec_bias": scatter_about(arg_keys[6], (D,), 0.5, 3.0, ((0, 2),), jnp.float32),
        "blocks": draw_blocks(jax.random.fold_in(jax.random.fold_in(arg_keys[9], part), 71), part),
        "counts": draw_counts(jax.random.fold_in(jax.random.fold_in(arg_keys[9], part), 71), part),
    }


band_width = 0.125


def reference(tokens, cotangent, enc_weight, enc_bias, threshold, dec_weight, dec_bias, blocks, counts):
    shard_count = N_LAT * N_SUB
    block_total = shard_count * BLK_DEV
    span = BPU * BLK
    x_tiles = tokens.astype(jnp.float32).reshape(TILES, TILE, D)
    g_tiles = cotangent.astype(jnp.float32).reshape(TILES, TILE, D)
    enc_blocks = enc_weight.reshape(D, block_total, BLK)
    dec_blocks = dec_weight.reshape(block_total, BLK, D)
    bias_blocks = enc_bias.reshape(block_total, BLK)
    level_blocks = threshold.reshape(block_total, BLK)
    slot_iota = lax.broadcasted_iota(jnp.int32, (TILES, BPU), 1)

    def one_shard(carry, shard):
        recon_sum, grad_sum = carry
        slot_ids = lax.dynamic_index_in_dim(blocks, shard, 1, keepdims=False)
        shard_counts = lax.dynamic_index_in_dim(counts, shard, 1, keepdims=True)
        live = (slot_iota < shard_counts).astype(jnp.float32)
        flat_ids = slot_ids.reshape(TILES * BPU).astype(jnp.int32)
        enc_sel = jnp.take(enc_blocks, flat_ids, axis=1).reshape(D, TILES, span).astype(jnp.float32)
        dec_sel = jnp.take(dec_blocks, flat_ids, axis=0).reshape(TILES, span, D).astype(jnp.float32)
        bias_sel = jnp.take(bias_blocks, flat_ids, axis=0).reshape(TILES, 1, span)
        level_sel = jnp.take(level_blocks, flat_ids, axis=0).reshape(TILES, 1, span)
        gate_mask = jnp.repeat(live, BLK, axis=1)[:, None, :]
        preact = jnp.einsum("tnd,dtl->tnl", x_tiles, enc_sel) + bias_sel
        grad_latent = jnp.einsum("tnd,tld->tnl", g_tiles, dec_sel)
        jump = gate_mask * jnp.clip((preact - level_sel) / band_width, 0.0, 1.0)
        active = preact * jump
        gated = grad_latent * jump
        scores = jnp.sum(active * grad_latent, axis=1)
        active_low = lax.optimization_barrier(active.astype(jnp.bfloat16)).astype(jnp.float32)
        gated_low = lax.optimization_barrier(gated.astype(jnp.bfloat16)).astype(jnp.float32)
        recon_sum = recon_sum + jnp.einsum("tnl,tld->tnd", active_low, dec_sel)
        grad_sum = grad_sum + jnp.einsum("tnl,dtl->tnd", gated_low, enc_sel)
        return (recon_sum, grad_sum), scores

    zeros = jnp.zeros((TILES, TILE, D), jnp.float32)
    (recon_sum, grad_sum), scores = lax.scan(one_shard, (zeros, zeros), jnp.arange(shard_count, dtype=jnp.int32))
    reconstruction = (recon_sum.reshape(TILES * TILE, D) + dec_bias).astype(jnp.bfloat16)
    input_grad = grad_sum.reshape(TILES * TILE, D).astype(jnp.bfloat16)
    flat_scores = scores.reshape(shard_count * TILES * BPU, BLK)
    all_ids = jnp.transpose(blocks, (1, 0, 2)).reshape(shard_count * TILES * BPU).astype(jnp.int32)
    attribution = jax.ops.segment_sum(flat_scores, all_ids, num_segments=block_total).reshape(block_total * BLK)
    return reconstruction, input_grad, attribution
```

```python
import functools

import jax
import jax.numpy as jnp
from jax import lax
from jax.experimental import pallas as pl
from jax.experimental.pallas import tpu as pltpu
from jax.sharding import PartitionSpec as P

BLK = 64


band_width = 0.125
MESH = pl.DeviceIdType.MESH
COL = 256


def split3(v):
    hi = v.astype(jnp.bfloat16)
    rest = v - hi.astype(jnp.float32)
    mid = rest.astype(jnp.bfloat16)
    low = (rest - mid.astype(jnp.float32)).astype(jnp.bfloat16)
    return hi, mid, low


def rows_of(parts, width):
    row = lax.broadcasted_iota(jnp.int32, (16, width), 0)
    out = jnp.zeros((16, width), jnp.float32)
    for i, part in enumerate(parts):
        out = jnp.where(row == i, part.astype(jnp.float32), out)
    return out.astype(jnp.bfloat16)


def near_first(n, me, k):
    out = 0
    for z in range(n):
        order = sorted(range(n), key=lambda t: (abs(t - z), t if z < n // 2 else -t))
        out = jnp.where(me == z, order[k], out)
    return out


def dot(a, b):
    return jnp.dot(a, b, preferred_element_type=jnp.float32)


def dot_t(a, b):
    return lax.dot_general(a, b, (((1,), (1,)), ((), ())), preferred_element_type=jnp.float32)


def kernel(n, dims,
           blocks_ref, counts_ref, tok_ref, cot_ref, enc_hbm, dec_hbm, bias_ref, level_ref, dbias_ref,
           recon_ref, grad_ref, attr_ref,
           enc, dec, xg, pick, stack, lat_stack, dense, xs_pre, xs_g, xr_pre, xr_g, side,
           keep, sib_out, sib_in, term, home, own,
           load_sem, z_send, z_recv, s_send, s_recv, xp_send, xp_recv, xq_send, xq_recv,
           b_send, b_recv, h_send, h_recv, f_send, f_recv):
    rows, width, latents, slots = dims
    span = slots * BLK
    z, x, c = lax.axis_index("lat"), lax.axis_index("dm"), lax.axis_index("sub")
    tiles = [near_first(n, z, k) for k in range(n)]
    other_c, other_x = 1 - c, 1 - x

    loads = [
        pltpu.make_async_copy(tok_ref, xg.at[0, z], load_sem.at[0]),
        pltpu.make_async_copy(cot_ref, xg.at[1, z], load_sem.at[1]),
        pltpu.make_async_copy(enc_hbm, enc, load_sem.at[2]),
        pltpu.make_async_copy(dec_hbm, dec, load_sem.at[3]),
    ]
    for load in loads:
        load.start()

    barrier = pltpu.get_barrier_semaphore()
    for k in range(1, n):
        pl.semaphore_signal(barrier, inc=1, device_id={"lat": tiles[k]}, device_id_type=MESH)
    pl.semaphore_signal(barrier, inc=1, device_id={"dm": other_x}, device_id_type=MESH)
    pl.semaphore_signal(barrier, inc=1, device_id={"sub": other_c}, device_id_type=MESH)
    pl.semaphore_wait(barrier, n + 1)

    def copy(src, dst, send, recv, to):
        return pltpu.make_async_remote_copy(
            src_ref=src, dst_ref=dst, send_sem=send, recv_sem=recv, device_id=to, device_id_type=MESH)

    ends = []

    def send_if(cond, desc):
        @pl.when(cond)
        def _():
            desc.start()

        def finish():
            @pl.when(cond)
            def _():
                desc.wait_send()
        ends.append(finish)

    def send(desc):
        desc.start()
        ends.append(desc.wait_send)

    def up(t, k):
        return copy(xg.at[c, t], xg.at[c, t], z_send.at[0, k], z_recv.at[t], {"lat": jnp.minimum(z + 1, n - 1)})

    def down(t, k):
        return copy(xg.at[c, t], xg.at[c, t], z_send.at[1, k], z_recv.at[t], {"lat": jnp.maximum(z - 1, 0)})

    loads[0].wait()
    loads[1].wait()
    send_if(z < n - 1, up(z, 0))
    send_if(z > 0, down(z, 0))

    b3 = split3(bias_ref[...])
    l3 = split3(level_ref[...])
    stack[3 * rows:, :] = rows_of(b3 + l3, latents)
    attr_ref[...] = jnp.zeros_like(attr_ref)
    loads[2].wait()
    loads[3].wait()

    def ingest(k):
        t = tiles[k]
        up(t, k).wait_recv()
        send_if((t < z) & (z < n - 1), up(t, k))
        send_if((t > z) & (z > 0), down(t, k))
        send(copy(xg.at[c, t], xg.at[c, t], s_send.at[k], s_recv.at[k], {"sub": other_c}))
        copy(xg.at[other_c, t], xg.at[other_c, t], s_send.at[k], s_recv.at[k], {"sub": other_c}).wait_recv()

    def partial(k):
        t = tiles[k]

        def first(i, carry):
            cols = pl.ds(pl.multiple_of(i * COL, COL), COL)
            p = dot(xg[0, t], enc[:, cols])
            hi = p.astype(jnp.bfloat16)
            stack[0:rows, cols] = hi
            stack[rows:2 * rows, cols] = (p - hi.astype(jnp.float32)).astype(jnp.bfloat16)
            stack[2 * rows:3 * rows, cols] = dot_t(xg[1, t], dec[cols, :]).astype(jnp.bfloat16)
            return carry

        lax.fori_loop(0, latents // COL, first, 0)

        lane = lax.broadcasted_iota(jnp.int32, (1, span), 1)
        slot = lane // BLK
        target = jnp.full((1, span), -1, jnp.int32)
        count = counts_ref[t, 0]
        for s in range(slots):
            base = jnp.where(s < count, (blocks_ref[t, s] % (latents // BLK)) * BLK, -2 * latents)
            target = jnp.where(slot == s, base + lane % BLK, target)
        for i in range(span // COL):
            cols = slice(i * COL, (i + 1) * COL)
            hit = lax.broadcasted_iota(jnp.int32, (latents, COL), 0) == target[:, cols]
            one = jnp.where(hit, 1.0, 0.0).astype(jnp.bfloat16)
            pick[k % 2, :, cols] = one
            r = dot(stack[...], one)
            xs_pre[k, :, cols] = r[0:rows] + r[rows:2 * rows]
            xs_g[k, :, cols] = r[2 * rows:3 * rows].astype(jnp.bfloat16)
            b = 3 * rows
            side[k, 0:1, cols] = r[b:b + 1] + r[b + 1:b + 2] + r[b + 2:b + 3]
            side[k, 1:2, cols] = r[b + 3:b + 4] + r[b + 4:b + 5] + r[b + 5:b + 6]
        send(copy(xs_pre.at[k], xr_pre.at[k], xp_send.at[k], xp_recv.at[k], {"dm": other_x}))
        send(copy(xs_g.at[k], xr_g.at[k], xq_send.at[k], xq_recv.at[k], {"dm": other_x}))

    def second(k):
        copy(xs_pre.at[k], xr_pre.at[k], xp_send.at[k], xp_recv.at[k], {"dm": other_x}).wait_recv()
        copy(xs_g.at[k], xr_g.at[k], xq_send.at[k], xq_recv.at[k], {"dm": other_x}).wait_recv()
        pre = xs_pre[k] + xr_pre[k] + side[k, 0:1, :]
        gl = xs_g[k].astype(jnp.float32) + xr_g[k].astype(jnp.float32)
        jump = jnp.clip((pre - side[k, 1:2, :]) / band_width, 0.0, 1.0)
        active = pre * jump
        lat_stack[0:rows, :] = active.astype(jnp.bfloat16)
        lat_stack[rows:2 * rows, :] = (gl * jump).astype(jnp.bfloat16)
        scores = jnp.sum(active * gl, axis=0, keepdims=True)
        lat_stack[2 * rows:, :] = rows_of(split3(scores), span)

        def spread(i, carry):
            cols = pl.ds(pl.multiple_of(i * COL, COL), COL)
            r = dot_t(lat_stack[...], pick[k % 2, cols, :])
            dense[:, cols] = r[0:2 * rows].astype(jnp.bfloat16)
            b = 2 * rows
            attr_ref[0:1, cols] += r[b:b + 1] + r[b + 1:b + 2] + r[b + 2:b + 3]
            return carry

        lax.fori_loop(0, latents // COL, spread, 0)

        def out(i, carry):
            cols = pl.ds(pl.multiple_of(i * COL, COL), COL)
            rec = dot(dense[0:rows, :], dec[:, cols])
            gra = dot_t(dense[rows:2 * rows, :], enc[cols, :])
            first_core = c == 0
            keep[k, :, cols] = jnp.where(first_core, rec, gra)
            sib_out[k, :, cols] = jnp.where(first_core, gra, rec).astype(jnp.bfloat16)
            return carry

        lax.fori_loop(0, width // COL, out, 0)
        send(copy(sib_out.at[k], sib_in.at[k], b_send.at[k], b_recv.at[k], {"sub": other_c}))

    def deliver(k):
        copy(sib_out.at[k], sib_in.at[k], b_send.at[k], b_recv.at[k], {"sub": other_c}).wait_recv()
        total = keep[k] + sib_in[k].astype(jnp.float32)
        if k == 0:
            own[...] = total
        else:
            term[k] = total.astype(jnp.bfloat16)
            send(copy(term.at[k], home.at[z], h_send.at[k], h_recv.at[z], {"lat": tiles[k]}))

    for k in range(n):
        if k:
            ingest(k)
        partial(k)
        if k >= 1:
            second(k - 1)
            deliver(k - 1)
    second(n - 1)
    deliver(n - 1)

    total = own[...] + jnp.where(c == 0, dbias_ref[...], 0.0)
    for k in range(1, n):
        s = tiles[k]
        copy(term.at[k], home.at[s], h_send.at[k], h_recv.at[s], {"lat": s}).wait_recv()
        total += home[s].astype(jnp.float32)
    final = total.astype(jnp.bfloat16)

    give_recon = copy(recon_ref, recon_ref, f_send.at[0], f_recv.at[0], {"sub": other_c})
    give_grad = copy(grad_ref, grad_ref, f_send.at[1], f_recv.at[1], {"sub": other_c})

    @pl.when(c == 0)
    def _():
        recon_ref[...] = final
        give_recon.start()
        give_grad.wait_recv()
        give_recon.wait_send()

    @pl.when(c == 1)
    def _():
        grad_ref[...] = final
        give_grad.start()
        give_recon.wait_recv()
        give_grad.wait_send()

    for finish in ends:
        finish()


def fused(n, tokens, cotangent, enc_weight, enc_bias, threshold, dec_weight, dec_bias, blocks, counts):
    rows, width = tokens.shape
    latents = enc_weight.shape[1]
    slots = blocks.shape[2]
    span = slots * BLK
    vmem, anywhere, smem = (pl.BlockSpec(memory_space=s) for s in (pltpu.VMEM, pl.ANY, pltpu.SMEM))
    bf, f32 = jnp.bfloat16, jnp.float32
    sem = pltpu.SemaphoreType.DMA
    flops = 2 * 4 * n * rows * width * latents
    recon, grad, attr = pl.pallas_call(
        functools.partial(kernel, n, (rows, width, latents, slots)),
        out_shape=(
            jax.ShapeDtypeStruct((rows, width), bf),
            jax.ShapeDtypeStruct((rows, width), bf),
            jax.ShapeDtypeStruct((1, latents), f32),
        ),
        in_specs=[smem, smem, anywhere, anywhere, anywhere, anywhere, vmem, vmem, vmem],
        out_specs=(vmem, vmem, vmem),
        scratch_shapes=[
            pltpu.VMEM((width, latents), bf),
            pltpu.VMEM((latents, width), bf),
            pltpu.VMEM((2, n, rows, width), bf),
            pltpu.VMEM((2, latents, span), bf),
            pltpu.VMEM((3 * rows + 16, latents), bf),
            pltpu.VMEM((2 * rows + 16, span), bf),
            pltpu.VMEM((2 * rows, latents), bf),
            pltpu.VMEM((n, rows, span), f32),
            pltpu.VMEM((n, rows, span), bf),
            pltpu.VMEM((n, rows, span), f32),
            pltpu.VMEM((n, rows, span), bf),
            pltpu.VMEM((n, 8, span), f32),
            pltpu.VMEM((n, rows, width), f32),
            pltpu.VMEM((n, rows, width), bf),
            pltpu.VMEM((n, rows, width), bf),
            pltpu.VMEM((n, rows, width), bf),
            pltpu.VMEM((n, rows, width), bf),
            pltpu.VMEM((rows, width), f32),
            sem((4,)), sem((2, n)), sem((n,)), sem((n,)), sem((n,)),
            sem((n,)), sem((n,)), sem((n,)), sem((n,)),
            sem((n,)), sem((n,)), sem((n,)), sem((n,)), sem((2,)), sem((2,)),
        ],
        compiler_params=pltpu.CompilerParams(
            collective_id=0, has_side_effects=True, vmem_limit_bytes=56 * 1024 * 1024),
        cost_estimate=pl.CostEstimate(flops=flops, bytes_accessed=4 * width * latents, transcendentals=0),
    )(blocks[:, 0, :], counts, tokens, cotangent, enc_weight, dec_weight,
      enc_bias[None, :], threshold[None, :], dec_bias[None, :])
    return recon, grad, attr[0]


def plain(tokens, cotangent, enc_weight, enc_bias, threshold, dec_weight, dec_bias, blocks, counts):
    whole_tokens, whole_grads = (
        lax.all_gather(tokens, "lat", axis=0, tiled=True),
        lax.all_gather(cotangent, "lat", axis=0, tiled=True),
    )
    tile_count = blocks.shape[0]
    slot_count = blocks.shape[2]
    width = tokens.shape[1]
    block_len = BLK
    block_count = enc_weight.shape[1] // block_len
    span = slot_count * block_len
    tile_len = whole_tokens.shape[0] // tile_count
    x_tiles = whole_tokens.reshape(tile_count, tile_len, width)
    g_tiles = whole_grads.reshape(tile_count, tile_len, width)
    flat_ids = (blocks[:, 0, :] % block_count).reshape(tile_count * slot_count)
    enc_sel = jnp.take(enc_weight.reshape(width, block_count, block_len), flat_ids, axis=1).reshape(
        width, tile_count, span
    )
    dec_sel = jnp.take(dec_weight.reshape(block_count, block_len, width), flat_ids, axis=0).reshape(
        tile_count, span, width
    )
    bias_sel = jnp.take(enc_bias.reshape(block_count, block_len), flat_ids, axis=0).reshape(
        tile_count, 1, span
    )
    level_sel = jnp.take(threshold.reshape(block_count, block_len), flat_ids, axis=0).reshape(
        tile_count, 1, span
    )
    live = (lax.broadcasted_iota(jnp.int32, (tile_count, slot_count), 1) < counts).astype(
        jnp.float32
    )
    gate_mask = jnp.repeat(live, block_len, axis=1)[:, None, :]
    enc_part = jnp.einsum("tnd,dtl->tnl", x_tiles, enc_sel, preferred_element_type=jnp.float32)
    dec_part = jnp.einsum("tnd,tld->tnl", g_tiles, dec_sel, preferred_element_type=jnp.float32)
    preact, grad_latent = lax.psum((enc_part, dec_part), "dm")
    preact = preact + bias_sel
    jump = gate_mask * jnp.clip((preact - level_sel) / band_width, 0.0, 1.0)
    active = preact * jump
    gated = grad_latent * jump
    scores = jnp.sum(active * grad_latent, axis=1)
    active_low = active.astype(jnp.bfloat16)
    gated_low = gated.astype(jnp.bfloat16)
    recon_rows = jnp.einsum(
        "tnl,tld->tnd", active_low, dec_sel, preferred_element_type=jnp.float32
    ).reshape(tile_count * tile_len, width)
    grad_rows = jnp.einsum(
        "tnl,dtl->tnd", gated_low, enc_sel, preferred_element_type=jnp.float32
    ).reshape(tile_count * tile_len, width)
    recon_part, grad_part = (
        lax.psum_scatter(recon_rows, "lat", scatter_dimension=0, tiled=True),
        lax.psum_scatter(grad_rows, "lat", scatter_dimension=0, tiled=True),
    )
    recon_full, grad_full = lax.psum((recon_part, grad_part), "sub")
    recon_out = (recon_full + dec_bias).astype(jnp.bfloat16)
    grad_out = grad_full.astype(jnp.bfloat16)
    picker = (
        flat_ids[:, None]
        == lax.broadcasted_iota(jnp.int32, (tile_count * slot_count, block_count), 1)
    ).astype(jnp.float32)
    slot_scores = scores.reshape(tile_count * slot_count, block_len)
    attribution = jnp.einsum(
        "sk,sb->kb",
        picker,
        slot_scores,
        precision=lax.Precision.HIGHEST,
        preferred_element_type=jnp.float32,
    ).reshape(block_count * block_len)
    return (recon_out, grad_out, attribution)


def solution(mesh):
    n = mesh.shape["lat"]

    def local(*args):
        tokens, blocks = args[0], args[7]
        if n == blocks.shape[0] and mesh.shape["dm"] == 2 and mesh.shape["sub"] == 2:
            return fused(n, *args)
        return plain(*args)

    in_specs = (
        P(("groups", "lat"), "dm"),
        P(("groups", "lat"), "dm"),
        P("dm", ("lat", "sub")),
        P(("lat", "sub")),
        P(("lat", "sub")),
        P(("lat", "sub"), "dm"),
        P("dm"),
        P("groups", ("lat", "sub"), None),
        P("groups", ("lat", "sub")),
    )
    out_specs = (
        P(("groups", "lat"), "dm"),
        P(("groups", "lat"), "dm"),
        P(("groups", "lat", "sub")),
    )
    return jax.shard_map(local, mesh=mesh, in_specs=in_specs, out_specs=out_specs, check_vma=False)
```

```python
import functools

import jax
import jax.numpy as jnp
from jax import lax
from jax.experimental import pallas as pl
from jax.experimental.pallas import tpu as pltpu
from jax.sharding import PartitionSpec as P

BLK = 64


band_width = 0.125
MESH = pl.DeviceIdType.MESH
COL = 256


def split3(v):
    hi = v.astype(jnp.bfloat16)
    rest = v - hi.astype(jnp.float32)
    mid = rest.astype(jnp.bfloat16)
    low = (rest - mid.astype(jnp.float32)).astype(jnp.bfloat16)
    return hi, mid, low


def rows_of(parts, width):
    row = lax.broadcasted_iota(jnp.int32, (16, width), 0)
    out = jnp.zeros((16, width), jnp.float32)
    for i, part in enumerate(parts):
        out = jnp.where(row == i, part.astype(jnp.float32), out)
    return out.astype(jnp.bfloat16)


def near_first(n, me, k):
    out = 0
    for z in range(n):
        order = sorted(range(n), key=lambda t: (abs(t - z), t if z < n // 2 else -t))
        out = jnp.where(me == z, order[k], out)
    return out


def dot(a, b):
    return jnp.dot(a, b, preferred_element_type=jnp.float32)


def dot_t(a, b):
    return lax.dot_general(a, b, (((1,), (1,)), ((), ())), preferred_element_type=jnp.float32)


def kernel(n, dims,
           blocks_ref, counts_ref, tok_ref, cot_ref, enc_hbm, dec_hbm, bias_ref, level_ref, dbias_ref,
           recon_ref, grad_ref, attr_ref,
           enc, dec, xg, back, stack, lat_stack, dense, xs, xr, scale_s, scale_r, side,
           keep, sib_out, sib_in, term, home, own,
           load_sem, z_send, z_recv, s_send, s_recv, xp_send, xp_recv, xq_send, xq_recv,
           b_send, b_recv, h_send, h_recv, f_send, f_recv):
    rows, width, latents, slots = dims
    span = slots * BLK
    z, x, c = lax.axis_index("lat"), lax.axis_index("dm"), lax.axis_index("sub")
    tiles = [near_first(n, z, k) for k in range(n)]
    other_c, other_x = 1 - c, 1 - x

    loads = [
        pltpu.make_async_copy(tok_ref, xg.at[0, z], load_sem.at[0]),
        pltpu.make_async_copy(cot_ref, xg.at[1, z], load_sem.at[1]),
        pltpu.make_async_copy(enc_hbm, enc, load_sem.at[2]),
        pltpu.make_async_copy(dec_hbm, dec, load_sem.at[3]),
    ]
    for load in loads:
        load.start()

    barrier = pltpu.get_barrier_semaphore()
    for k in range(1, n):
        pl.semaphore_signal(barrier, inc=1, device_id={"lat": tiles[k]}, device_id_type=MESH)
    pl.semaphore_signal(barrier, inc=1, device_id={"dm": other_x}, device_id_type=MESH)
    pl.semaphore_signal(barrier, inc=1, device_id={"sub": other_c}, device_id_type=MESH)
    pl.semaphore_wait(barrier, n + 1)

    def copy(src, dst, send, recv, to):
        return pltpu.make_async_remote_copy(
            src_ref=src, dst_ref=dst, send_sem=send, recv_sem=recv, device_id=to, device_id_type=MESH)

    ends = []

    def send_if(cond, desc):
        @pl.when(cond)
        def _():
            desc.start()

        def finish():
            @pl.when(cond)
            def _():
                desc.wait_send()
        ends.append(finish)

    def send(desc):
        desc.start()
        ends.append(desc.wait_send)

    def up(t, k):
        return copy(xg.at[c, t], xg.at[c, t], z_send.at[0, k], z_recv.at[t], {"lat": jnp.minimum(z + 1, n - 1)})

    def down(t, k):
        return copy(xg.at[c, t], xg.at[c, t], z_send.at[1, k], z_recv.at[t], {"lat": jnp.maximum(z - 1, 0)})

    loads[0].wait()
    loads[1].wait()
    send_if(z < n - 1, up(z, 0))
    send_if(z > 0, down(z, 0))

    b3 = split3(bias_ref[...])
    l3 = split3(level_ref[...])
    stack[4 * rows:, :] = rows_of(b3 + l3, latents)
    scale_s[...] = jnp.zeros_like(scale_s)
    attr_ref[...] = jnp.zeros_like(attr_ref)
    loads[2].wait()
    loads[3].wait()

    def take_in(k):
        t = tiles[k]
        up(t, k).wait_recv()
        send_if((t < z) & (z < n - 1), up(t, k))
        send_if((t > z) & (z > 0), down(t, k))
        send(copy(xg.at[c, t], xg.at[c, t], s_send.at[k], s_recv.at[k], {"sub": other_c}))

    def take_pair(k):
        t = tiles[k]
        copy(xg.at[other_c, t], xg.at[other_c, t], s_send.at[k], s_recv.at[k], {"sub": other_c}).wait_recv()

    def code(v):
        top = jnp.max(jnp.abs(v), axis=0, keepdims=True)
        grow = jnp.where(top > 1e-30, 32767.0 / jnp.maximum(top, 1e-30), 0.0)
        return jnp.round(v * grow).astype(jnp.int32).astype(jnp.int16), top * (1.0 / 32767.0)

    def swap(k, i):
        return (copy(xs.at[k, i], xr.at[k, i], xp_send.at[k, i], xp_recv.at[k, i], {"dm": other_x}),
                copy(scale_s.at[k, i], scale_r.at[k, i], xq_send.at[k, i], xq_recv.at[k, i], {"dm": other_x}))

    def partial(k):
        t = tiles[k]

        def first(i, carry):
            cols = pl.ds(pl.multiple_of(i * COL, COL), COL)
            p = dot(xg[0, t], enc[:, cols])
            hi = p.astype(jnp.bfloat16)
            stack[0:rows, cols] = hi
            stack[rows:2 * rows, cols] = (p - hi.astype(jnp.float32)).astype(jnp.bfloat16)
            q = dot_t(xg[1, t], dec[cols, :])
            hi = q.astype(jnp.bfloat16)
            stack[2 * rows:3 * rows, cols] = hi
            stack[3 * rows:4 * rows, cols] = (q - hi.astype(jnp.float32)).astype(jnp.bfloat16)
            return carry

        lax.fori_loop(0, latents // COL, first, 0)

        lane = lax.broadcasted_iota(jnp.int32, (1, span), 1)
        slot = lane // BLK
        target = jnp.full((1, span), -1, jnp.int32)
        count = counts_ref[t, 0]
        across = (lax.broadcasted_iota(jnp.int32, (BLK, latents), 1)
                  - lax.broadcasted_iota(jnp.int32, (BLK, latents), 0))
        for s in range(slots):
            base = jnp.where(s < count, (blocks_ref[t, s] % (latents // BLK)) * BLK, -2 * latents)
            target = jnp.where(slot == s, base + lane % BLK, target)
            back[k % 2, s * BLK:(s + 1) * BLK, :] = jnp.where(across == base, 1.0, 0.0).astype(jnp.bfloat16)
        for i in range(span // COL):
            cols = slice(i * COL, (i + 1) * COL)
            hit = lax.broadcasted_iota(jnp.int32, (latents, COL), 0) == target[:, cols]
            one = jnp.where(hit, 1.0, 0.0).astype(jnp.bfloat16)
            r = dot(stack[...], one)
            xs[k, i, 0], scale_s[k, i, 0:1, :] = code(r[0:rows] + r[rows:2 * rows])
            xs[k, i, 1], scale_s[k, i, 1:2, :] = code(r[2 * rows:3 * rows] + r[3 * rows:4 * rows])
            for desc in swap(k, i):
                send(desc)
            b = 4 * rows
            side[k, i, 0:1, :] = r[b:b + 1] + r[b + 1:b + 2] + r[b + 2:b + 3]
            side[k, i, 1:2, :] = r[b + 3:b + 4] + r[b + 4:b + 5] + r[b + 5:b + 6]

    def whole(k, i, j):
        return (xs[k, i, j].astype(jnp.int32).astype(jnp.float32) * scale_s[k, i, j:j + 1, :]
                + xr[k, i, j].astype(jnp.int32).astype(jnp.float32) * scale_r[k, i, j:j + 1, :])

    def rec(cols):
        return dot(dense[0:rows, :], dec[:, cols])

    def gra(cols):
        return dot_t(dense[rows:2 * rows, :], enc[cols, :])

    def for_columns(store, form):
        def body(i, carry):
            cols = pl.ds(pl.multiple_of(i * COL, COL), COL)
            store(cols, form(cols))
            return carry
        lax.fori_loop(0, width // COL, body, 0)

    def by_core(store, forms):
        for core in range(2):
            @pl.when(c == core)
            def _():
                for_columns(store, forms[core])

    def second(k):
        for i in range(span // COL):
            cols = slice(i * COL, (i + 1) * COL)
            for desc in swap(k, i):
                desc.wait_recv()
            pre = whole(k, i, 0) + side[k, i, 0:1, :]
            gl = whole(k, i, 1)
            jump = jnp.clip((pre - side[k, i, 1:2, :]) / band_width, 0.0, 1.0)
            active = pre * jump
            lat_stack[0:rows, cols] = active.astype(jnp.bfloat16)
            lat_stack[rows:2 * rows, cols] = (gl * jump).astype(jnp.bfloat16)
            scores = jnp.sum(active * gl, axis=0, keepdims=True)
            lat_stack[2 * rows:, cols] = rows_of(split3(scores), COL)

        def spread(i, carry):
            cols = pl.ds(pl.multiple_of(i * COL, COL), COL)
            r = dot(lat_stack[...], back[k % 2, :, cols])
            dense[:, cols] = r[0:2 * rows].astype(jnp.bfloat16)
            b = 2 * rows
            attr_ref[0:1, cols] += r[b:b + 1] + r[b + 1:b + 2] + r[b + 2:b + 3]
            return carry

        lax.fori_loop(0, latents // COL, spread, 0)

        def store(cols, v):
            sib_out[k, :, cols] = v.astype(jnp.bfloat16)

        by_core(store, (gra, rec))
        send(copy(sib_out.at[k], sib_in.at[k], b_send.at[k], b_recv.at[k], {"sub": other_c}))

    def deliver(k):
        def store(cols, v):
            keep[:, cols] = v

        by_core(store, (rec, gra))
        copy(sib_out.at[k], sib_in.at[k], b_send.at[k], b_recv.at[k], {"sub": other_c}).wait_recv()
        total = keep[...] + sib_in[k].astype(jnp.float32)
        if k == 0:
            own[...] = total
        else:
            term[k] = total.astype(jnp.bfloat16)
            send(copy(term.at[k], home.at[z], h_send.at[k], h_recv.at[z], {"lat": tiles[k]}))

    for k in range(n):
        if k:
            take_pair(k)
        partial(k)
        if k:
            second(k - 1)
        if k + 1 < n:
            take_in(k + 1)
        if k:
            deliver(k - 1)
    second(n - 1)
    deliver(n - 1)

    total = own[...] + jnp.where(c == 0, dbias_ref[...], 0.0)
    for k in range(1, n):
        s = tiles[k]
        copy(term.at[k], home.at[s], h_send.at[k], h_recv.at[s], {"lat": s}).wait_recv()
        total += home[s].astype(jnp.float32)
    final = total.astype(jnp.bfloat16)

    give_recon = copy(recon_ref, recon_ref, f_send.at[0], f_recv.at[0], {"sub": other_c})
    give_grad = copy(grad_ref, grad_ref, f_send.at[1], f_recv.at[1], {"sub": other_c})

    @pl.when(c == 0)
    def _():
        recon_ref[...] = final
        give_recon.start()
        give_grad.wait_recv()
        give_recon.wait_send()

    @pl.when(c == 1)
    def _():
        grad_ref[...] = final
        give_grad.start()
        give_recon.wait_recv()
        give_grad.wait_send()

    for finish in ends:
        finish()


def fused(n, tokens, cotangent, enc_weight, enc_bias, threshold, dec_weight, dec_bias, blocks, counts):
    rows, width = tokens.shape
    latents = enc_weight.shape[1]
    slots = blocks.shape[2]
    span = slots * BLK
    parts = span // COL
    vmem, anywhere, smem = (pl.BlockSpec(memory_space=s) for s in (pltpu.VMEM, pl.ANY, pltpu.SMEM))
    bf, f32 = jnp.bfloat16, jnp.float32
    sem = pltpu.SemaphoreType.DMA
    flops = 2 * 4 * n * rows * width * latents
    recon, grad, attr = pl.pallas_call(
        functools.partial(kernel, n, (rows, width, latents, slots)),
        out_shape=(
            jax.ShapeDtypeStruct((rows, width), bf),
            jax.ShapeDtypeStruct((rows, width), bf),
            jax.ShapeDtypeStruct((1, latents), f32),
        ),
        in_specs=[smem, smem, anywhere, anywhere, anywhere, anywhere, vmem, vmem, vmem],
        out_specs=(vmem, vmem, vmem),
        scratch_shapes=[
            pltpu.VMEM((width, latents), bf),
            pltpu.VMEM((latents, width), bf),
            pltpu.VMEM((2, n, rows, width), bf),
            pltpu.VMEM((2, span, latents), bf),
            pltpu.VMEM((4 * rows + 16, latents), bf),
            pltpu.VMEM((2 * rows + 16, span), bf),
            pltpu.VMEM((2 * rows, latents), bf),
            pltpu.VMEM((n, parts, 2, rows, COL), jnp.int16),
            pltpu.VMEM((n, parts, 2, rows, COL), jnp.int16),
            pltpu.VMEM((n, parts, 8, COL), f32),
            pltpu.VMEM((n, parts, 8, COL), f32),
            pltpu.VMEM((n, parts, 8, COL), f32),
            pltpu.VMEM((rows, width), f32),
            pltpu.VMEM((n, rows, width), bf),
            pltpu.VMEM((n, rows, width), bf),
            pltpu.VMEM((n, rows, width), bf),
            pltpu.VMEM((n, rows, width), bf),
            pltpu.VMEM((rows, width), f32),
            sem((4,)), sem((2, n)), sem((n,)), sem((n,)), sem((n,)),
            sem((n, parts)), sem((n, parts)), sem((n, parts)), sem((n, parts)),
            sem((n,)), sem((n,)), sem((n,)), sem((n,)), sem((2,)), sem((2,)),
        ],
        compiler_params=pltpu.CompilerParams(
            collective_id=0, has_side_effects=True, vmem_limit_bytes=56 * 1024 * 1024),
        cost_estimate=pl.CostEstimate(flops=flops, bytes_accessed=4 * width * latents, transcendentals=0),
    )(blocks[:, 0, :], counts, tokens, cotangent, enc_weight, dec_weight,
      enc_bias[None, :], threshold[None, :], dec_bias[None, :])
    return recon, grad, attr[0]


def plain(tokens, cotangent, enc_weight, enc_bias, threshold, dec_weight, dec_bias, blocks, counts):
    whole_tokens, whole_grads = (
        lax.all_gather(tokens, "lat", axis=0, tiled=True),
        lax.all_gather(cotangent, "lat", axis=0, tiled=True),
    )
    tile_count = blocks.shape[0]
    slot_count = blocks.shape[2]
    width = tokens.shape[1]
    block_len = BLK
    block_count = enc_weight.shape[1] // block_len
    span = slot_count * block_len
    tile_len = whole_tokens.shape[0] // tile_count
    x_tiles = whole_tokens.reshape(tile_count, tile_len, width)
    g_tiles = whole_grads.reshape(tile_count, tile_len, width)
    flat_ids = (blocks[:, 0, :] % block_count).reshape(tile_count * slot_count)
    enc_sel = jnp.take(enc_weight.reshape(width, block_count, block_len), flat_ids, axis=1).reshape(
        width, tile_count, span
    )
    dec_sel = jnp.take(dec_weight.reshape(block_count, block_len, width), flat_ids, axis=0).reshape(
        tile_count, span, width
    )
    bias_sel = jnp.take(enc_bias.reshape(block_count, block_len), flat_ids, axis=0).reshape(
        tile_count, 1, span
    )
    level_sel = jnp.take(threshold.reshape(block_count, block_len), flat_ids, axis=0).reshape(
        tile_count, 1, span
    )
    live = (lax.broadcasted_iota(jnp.int32, (tile_count, slot_count), 1) < counts).astype(
        jnp.float32
    )
    gate_mask = jnp.repeat(live, block_len, axis=1)[:, None, :]
    enc_part = jnp.einsum("tnd,dtl->tnl", x_tiles, enc_sel, preferred_element_type=jnp.float32)
    dec_part = jnp.einsum("tnd,tld->tnl", g_tiles, dec_sel, preferred_element_type=jnp.float32)
    preact, grad_latent = lax.psum((enc_part, dec_part), "dm")
    preact = preact + bias_sel
    jump = gate_mask * jnp.clip((preact - level_sel) / band_width, 0.0, 1.0)
    active = preact * jump
    gated = grad_latent * jump
    scores = jnp.sum(active * grad_latent, axis=1)
    active_low = active.astype(jnp.bfloat16)
    gated_low = gated.astype(jnp.bfloat16)
    recon_rows = jnp.einsum(
        "tnl,tld->tnd", active_low, dec_sel, preferred_element_type=jnp.float32
    ).reshape(tile_count * tile_len, width)
    grad_rows = jnp.einsum(
        "tnl,dtl->tnd", gated_low, enc_sel, preferred_element_type=jnp.float32
    ).reshape(tile_count * tile_len, width)
    recon_part, grad_part = (
        lax.psum_scatter(recon_rows, "lat", scatter_dimension=0, tiled=True),
        lax.psum_scatter(grad_rows, "lat", scatter_dimension=0, tiled=True),
    )
    recon_full, grad_full = lax.psum((recon_part, grad_part), "sub")
    recon_out = (recon_full + dec_bias).astype(jnp.bfloat16)
    grad_out = grad_full.astype(jnp.bfloat16)
    picker = (
        flat_ids[:, None]
        == lax.broadcasted_iota(jnp.int32, (tile_count * slot_count, block_count), 1)
    ).astype(jnp.float32)
    slot_scores = scores.reshape(tile_count * slot_count, block_len)
    attribution = jnp.einsum(
        "sk,sb->kb",
        picker,
        slot_scores,
        precision=lax.Precision.HIGHEST,
        preferred_element_type=jnp.float32,
    ).reshape(block_count * block_len)
    return (recon_out, grad_out, attribution)


def solution(mesh):
    n = mesh.shape["lat"]

    def local(*args):
        tokens, blocks = args[0], args[7]
        if n == blocks.shape[0] and mesh.shape["dm"] == 2 and mesh.shape["sub"] == 2:
            return fused(n, *args)
        return plain(*args)

    in_specs = (
        P(("groups", "lat"), "dm"),
        P(("groups", "lat"), "dm"),
        P("dm", ("lat", "sub")),
        P(("lat", "sub")),
        P(("lat", "sub")),
        P(("lat", "sub"), "dm"),
        P("dm"),
        P("groups", ("lat", "sub"), None),
        P("groups", ("lat", "sub")),
    )
    out_specs = (
        P(("groups", "lat"), "dm"),
        P(("groups", "lat"), "dm"),
        P(("groups", "lat", "sub")),
    )
    return jax.shard_map(local, mesh=mesh, in_specs=in_specs, out_specs=out_specs, check_vma=False)
```

```python
import functools

import jax
import jax.numpy as jnp
from jax import lax
from jax.experimental import pallas as pl
from jax.experimental.pallas import tpu as pltpu
from jax.sharding import PartitionSpec as P

BLK = 64


band_width = 0.125
MESH = pl.DeviceIdType.MESH
COL = 256


def split3(v):
    hi = v.astype(jnp.bfloat16)
    rest = v - hi.astype(jnp.float32)
    mid = rest.astype(jnp.bfloat16)
    low = (rest - mid.astype(jnp.float32)).astype(jnp.bfloat16)
    return hi, mid, low


def rows_of(parts, width):
    row = lax.broadcasted_iota(jnp.int32, (16, width), 0)
    out = jnp.zeros((16, width), jnp.float32)
    for i, part in enumerate(parts):
        out = jnp.where(row == i, part.astype(jnp.float32), out)
    return out.astype(jnp.bfloat16)


def near_first(n, me, k):
    out = 0
    for z in range(n):
        order = sorted(range(n), key=lambda t: (abs(t - z), t if z < n // 2 else -t))
        out = jnp.where(me == z, order[k], out)
    return out


def dot(a, b):
    return jnp.dot(a, b, preferred_element_type=jnp.float32)


def dot_t(a, b):
    return lax.dot_general(a, b, (((1,), (1,)), ((), ())), preferred_element_type=jnp.float32)


def kernel(n, dims,
           blocks_ref, counts_ref, tok_ref, cot_ref, enc_hbm, dec_hbm, bias_ref, level_ref, dbias_ref,
           recon_ref, grad_ref, attr_ref,
           enc, dec, xg, back, stack, lat_stack, dense, xs, xr, scale_s, scale_r, side,
           keep, sib_out, sib_in, term, home, own,
           load_sem, z_send, z_recv, s_send, s_recv, xp_send, xp_recv, xq_send, xq_recv,
           b_send, b_recv, h_send, h_recv, f_send, f_recv):
    rows, width, latents, slots = dims
    span = slots * BLK
    z, x, c = lax.axis_index("lat"), lax.axis_index("dm"), lax.axis_index("sub")
    tiles = [near_first(n, z, k) for k in range(n)]
    other_c, other_x = 1 - c, 1 - x

    loads = [
        pltpu.make_async_copy(tok_ref, xg.at[0, z], load_sem.at[0]),
        pltpu.make_async_copy(cot_ref, xg.at[1, z], load_sem.at[1]),
        pltpu.make_async_copy(enc_hbm, enc, load_sem.at[2]),
        pltpu.make_async_copy(dec_hbm, dec, load_sem.at[3]),
    ]
    for load in loads:
        load.start()

    barrier = pltpu.get_barrier_semaphore()
    for k in range(1, n):
        pl.semaphore_signal(barrier, inc=1, device_id={"lat": tiles[k]}, device_id_type=MESH)
    pl.semaphore_signal(barrier, inc=1, device_id={"dm": other_x}, device_id_type=MESH)
    pl.semaphore_signal(barrier, inc=1, device_id={"sub": other_c}, device_id_type=MESH)
    pl.semaphore_wait(barrier, n + 1)

    def copy(src, dst, send, recv, to):
        return pltpu.make_async_remote_copy(
            src_ref=src, dst_ref=dst, send_sem=send, recv_sem=recv, device_id=to, device_id_type=MESH)

    ends = []

    def send_if(cond, desc):
        @pl.when(cond)
        def _():
            desc.start()

        def finish():
            @pl.when(cond)
            def _():
                desc.wait_send()
        ends.append(finish)

    def send(desc):
        desc.start()
        ends.append(desc.wait_send)

    def up(t, k):
        return copy(xg.at[c, t], xg.at[c, t], z_send.at[0, k], z_recv.at[t], {"lat": jnp.minimum(z + 1, n - 1)})

    def down(t, k):
        return copy(xg.at[c, t], xg.at[c, t], z_send.at[1, k], z_recv.at[t], {"lat": jnp.maximum(z - 1, 0)})

    loads[0].wait()
    loads[1].wait()
    send_if(z < n - 1, up(z, 0))
    send_if(z > 0, down(z, 0))

    b3 = split3(bias_ref[...])
    l3 = split3(level_ref[...])
    stack[4 * rows:, :] = rows_of(b3 + l3, latents)
    scale_s[...] = jnp.zeros_like(scale_s)
    attr_ref[...] = jnp.zeros_like(attr_ref)
    loads[2].wait()
    loads[3].wait()

    def take_in(k):
        t = tiles[k]
        up(t, k).wait_recv()
        send_if((t < z) & (z < n - 1), up(t, k))
        send_if((t > z) & (z > 0), down(t, k))
        send(copy(xg.at[c, t], xg.at[c, t], s_send.at[k], s_recv.at[k], {"sub": other_c}))

    def take_pair(k):
        t = tiles[k]
        copy(xg.at[other_c, t], xg.at[other_c, t], s_send.at[k], s_recv.at[k], {"sub": other_c}).wait_recv()

    def code(v):
        top = jnp.max(jnp.abs(v), axis=0, keepdims=True)
        grow = jnp.where(top > 1e-30, 32767.0 / jnp.maximum(top, 1e-30), 0.0)
        return jnp.round(v * grow).astype(jnp.int32).astype(jnp.int16), top * (1.0 / 32767.0)

    def swap(k, i):
        return (copy(xs.at[k, i], xr.at[k, i], xp_send.at[k, i], xp_recv.at[k, i], {"dm": other_x}),
                copy(scale_s.at[k, i], scale_r.at[k, i], xq_send.at[k, i], xq_recv.at[k, i], {"dm": other_x}))

    def partial(k):
        t = tiles[k]

        def first(i, carry):
            cols = pl.ds(pl.multiple_of(i * COL, COL), COL)
            p = dot(xg[0, t], enc[:, cols])
            hi = p.astype(jnp.bfloat16)
            stack[0:rows, cols] = hi
            stack[rows:2 * rows, cols] = (p - hi.astype(jnp.float32)).astype(jnp.bfloat16)
            q = dot_t(xg[1, t], dec[cols, :])
            hi = q.astype(jnp.bfloat16)
            stack[2 * rows:3 * rows, cols] = hi
            stack[3 * rows:4 * rows, cols] = (q - hi.astype(jnp.float32)).astype(jnp.bfloat16)
            return carry

        lax.fori_loop(0, latents // COL, first, 0)

        lane = lax.broadcasted_iota(jnp.int32, (1, span), 1)
        slot = lane // BLK
        target = jnp.full((1, span), -1, jnp.int32)
        count = counts_ref[t, 0]
        across = (lax.broadcasted_iota(jnp.int32, (BLK, latents), 1)
                  - lax.broadcasted_iota(jnp.int32, (BLK, latents), 0))
        for s in range(slots):
            base = jnp.where(s < count, (blocks_ref[t, s] % (latents // BLK)) * BLK, -2 * latents)
            target = jnp.where(slot == s, base + lane % BLK, target)
            back[k % 2, s * BLK:(s + 1) * BLK, :] = jnp.where(across == base, 1.0, 0.0).astype(jnp.bfloat16)
        for i in range(span // COL):
            cols = slice(i * COL, (i + 1) * COL)
            hit = lax.broadcasted_iota(jnp.int32, (latents, COL), 0) == target[:, cols]
            one = jnp.where(hit, 1.0, 0.0).astype(jnp.bfloat16)
            r = dot(stack[...], one)
            xs[k, i, 0], scale_s[k, i, 0:1, :] = code(r[0:rows] + r[rows:2 * rows])
            xs[k, i, 1], scale_s[k, i, 1:2, :] = code(r[2 * rows:3 * rows] + r[3 * rows:4 * rows])
            for desc in swap(k, i):
                send(desc)
            b = 4 * rows
            side[k, i, 0:1, :] = r[b:b + 1] + r[b + 1:b + 2] + r[b + 2:b + 3]
            side[k, i, 1:2, :] = r[b + 3:b + 4] + r[b + 4:b + 5] + r[b + 5:b + 6]

    def whole(k, i, j):
        return (xs[k, i, j].astype(jnp.int32).astype(jnp.float32) * scale_s[k, i, j:j + 1, :]
                + xr[k, i, j].astype(jnp.int32).astype(jnp.float32) * scale_r[k, i, j:j + 1, :])

    def rec(cols):
        return dot(dense[0:rows, :], dec[:, cols])

    def gra(cols):
        return dot_t(dense[rows:2 * rows, :], enc[cols, :])

    def for_columns(store, form):
        def body(i, carry):
            cols = pl.ds(pl.multiple_of(i * COL, COL), COL)
            store(cols, form(cols))
            return carry
        lax.fori_loop(0, width // COL, body, 0)

    def by_core(store, forms):
        for core in range(2):
            @pl.when(c == core)
            def _():
                for_columns(store, forms[core])

    def second(k):
        for i in range(span // COL):
            cols = slice(i * COL, (i + 1) * COL)
            for desc in swap(k, i):
                desc.wait_recv()
            pre = whole(k, i, 0) + side[k, i, 0:1, :]
            gl = whole(k, i, 1)
            jump = jnp.clip((pre - side[k, i, 1:2, :]) / band_width, 0.0, 1.0)
            active = pre * jump
            lat_stack[0:rows, cols] = active.astype(jnp.bfloat16)
            lat_stack[rows:2 * rows, cols] = (gl * jump).astype(jnp.bfloat16)
            scores = jnp.sum(active * gl, axis=0, keepdims=True)
            lat_stack[2 * rows:, cols] = rows_of(split3(scores), COL)

        def spread(i, carry):
            cols = pl.ds(pl.multiple_of(i * COL, COL), COL)
            r = dot(lat_stack[...], back[k % 2, :, cols])
            dense[:, cols] = r[0:2 * rows].astype(jnp.bfloat16)
            b = 2 * rows
            attr_ref[0:1, cols] += r[b:b + 1] + r[b + 1:b + 2] + r[b + 2:b + 3]
            return carry

        lax.fori_loop(0, latents // COL, spread, 0)

        def store(cols, v):
            sib_out[k, :, cols] = v.astype(jnp.bfloat16)

        by_core(store, (gra, rec))
        send(copy(sib_out.at[k], sib_in.at[k], b_send.at[k], b_recv.at[k], {"sub": other_c}))

    def fed(k):
        t = tiles[k]
        return ((t > z) & (z > 0)) | ((t < z) & (z < n - 1))

    def landing(slot, j):
        return home.at[slot, j]

    def onward(k, j):
        t = tiles[k]
        step = jnp.where(t > z, z + 1, z - 1)
        slot = jnp.where(t == z + 1, n, t)
        return copy(term.at[k, j], landing(slot, j), h_send.at[k, j], h_recv.at[slot, j], {"lat": step})

    def arrived(slot, j):
        to = jnp.where(z > 0, z - 1, z + 1)
        copy(term.at[1, j], landing(slot, j), h_send.at[1, j], h_recv.at[slot, j], {"lat": to}).wait_recv()
        return home[slot, j].astype(jnp.float32)

    def relay(k, j):
        @pl.when(fed(k))
        def _():
            term[k, j] = (term[k, j].astype(jnp.float32) + arrived(tiles[k], j)).astype(jnp.bfloat16)
            onward(k, j).start()

    def deliver(k):
        def store(cols, v):
            keep[:, cols] = v

        by_core(store, (rec, gra))
        copy(sib_out.at[k], sib_in.at[k], b_send.at[k], b_recv.at[k], {"sub": other_c}).wait_recv()
        total = keep[...] + sib_in[k].astype(jnp.float32)
        if k == 0:
            own[...] = total
        else:
            for j in range(width // COL):
                term[k, j] = total[:, j * COL:(j + 1) * COL].astype(jnp.bfloat16)


            @pl.when(jnp.logical_not(fed(k)))
            def _():
                for j in range(width // COL):
                    onward(k, j).start()

    for k in range(n):
        if k:
            take_pair(k)
        partial(k)
        if k:
            second(k - 1)
        if k + 1 < n:
            take_in(k + 1)
        if k:
            deliver(k - 1)
    second(n - 1)
    for j in range(width // COL):
        relay(2, j)
    deliver(n - 1)
    for j in range(width // COL):
        relay(3, j)
        relay(1, j)

    for there, slot in ((z > 0, n), (z < n - 1, z)):
        @pl.when(there)
        def _():
            for j in range(width // COL):
                own[:, j * COL:(j + 1) * COL] += arrived(slot, j)
    total = own[...] + jnp.where(c == 0, dbias_ref[...], 0.0)
    final = total.astype(jnp.bfloat16)

    give_recon = copy(recon_ref, recon_ref, f_send.at[0], f_recv.at[0], {"sub": other_c})
    give_grad = copy(grad_ref, grad_ref, f_send.at[1], f_recv.at[1], {"sub": other_c})

    @pl.when(c == 0)
    def _():
        recon_ref[...] = final
        give_recon.start()
        give_grad.wait_recv()
        give_recon.wait_send()

    @pl.when(c == 1)
    def _():
        grad_ref[...] = final
        give_grad.start()
        give_recon.wait_recv()
        give_grad.wait_send()

    for k in range(1, n):
        for j in range(width // COL):
            onward(k, j).wait_send()
    for finish in ends:
        finish()


def fused(n, tokens, cotangent, enc_weight, enc_bias, threshold, dec_weight, dec_bias, blocks, counts):
    rows, width = tokens.shape
    latents = enc_weight.shape[1]
    slots = blocks.shape[2]
    span = slots * BLK
    parts = span // COL
    vmem, anywhere, smem = (pl.BlockSpec(memory_space=s) for s in (pltpu.VMEM, pl.ANY, pltpu.SMEM))
    bf, f32 = jnp.bfloat16, jnp.float32
    sem = pltpu.SemaphoreType.DMA
    flops = 2 * 4 * n * rows * width * latents
    recon, grad, attr = pl.pallas_call(
        functools.partial(kernel, n, (rows, width, latents, slots)),
        out_shape=(
            jax.ShapeDtypeStruct((rows, width), bf),
            jax.ShapeDtypeStruct((rows, width), bf),
            jax.ShapeDtypeStruct((1, latents), f32),
        ),
        in_specs=[smem, smem, anywhere, anywhere, anywhere, anywhere, vmem, vmem, vmem],
        out_specs=(vmem, vmem, vmem),
        scratch_shapes=[
            pltpu.VMEM((width, latents), bf),
            pltpu.VMEM((latents, width), bf),
            pltpu.VMEM((2, n, rows, width), bf),
            pltpu.VMEM((2, span, latents), bf),
            pltpu.VMEM((4 * rows + 16, latents), bf),
            pltpu.VMEM((2 * rows + 16, span), bf),
            pltpu.VMEM((2 * rows, latents), bf),
            pltpu.VMEM((n, parts, 2, rows, COL), jnp.int16),
            pltpu.VMEM((n, parts, 2, rows, COL), jnp.int16),
            pltpu.VMEM((n, parts, 8, COL), f32),
            pltpu.VMEM((n, parts, 8, COL), f32),
            pltpu.VMEM((n, parts, 8, COL), f32),
            pltpu.VMEM((rows, width), f32),
            pltpu.VMEM((n, rows, width), bf),
            pltpu.VMEM((n, rows, width), bf),
            pltpu.VMEM((n, width // COL, rows, COL), bf),
            pltpu.VMEM((n + 1, width // COL, rows, COL), bf),
            pltpu.VMEM((rows, width), f32),
            sem((4,)), sem((2, n)), sem((n,)), sem((n,)), sem((n,)),
            sem((n, parts)), sem((n, parts)), sem((n, parts)), sem((n, parts)),
            sem((n,)), sem((n,)), sem((n, width // COL)), sem((n + 1, width // COL)), sem((2,)), sem((2,)),
        ],
        compiler_params=pltpu.CompilerParams(
            collective_id=0, has_side_effects=True, vmem_limit_bytes=56 * 1024 * 1024),
        cost_estimate=pl.CostEstimate(flops=flops, bytes_accessed=4 * width * latents, transcendentals=0),
    )(blocks[:, 0, :], counts, tokens, cotangent, enc_weight, dec_weight,
      enc_bias[None, :], threshold[None, :], dec_bias[None, :])
    return recon, grad, attr[0]


def plain(tokens, cotangent, enc_weight, enc_bias, threshold, dec_weight, dec_bias, blocks, counts):
    whole_tokens, whole_grads = (
        lax.all_gather(tokens, "lat", axis=0, tiled=True),
        lax.all_gather(cotangent, "lat", axis=0, tiled=True),
    )
    tile_count = blocks.shape[0]
    slot_count = blocks.shape[2]
    width = tokens.shape[1]
    block_len = BLK
    block_count = enc_weight.shape[1] // block_len
    span = slot_count * block_len
    tile_len = whole_tokens.shape[0] // tile_count
    x_tiles = whole_tokens.reshape(tile_count, tile_len, width)
    g_tiles = whole_grads.reshape(tile_count, tile_len, width)
    flat_ids = (blocks[:, 0, :] % block_count).reshape(tile_count * slot_count)
    enc_sel = jnp.take(enc_weight.reshape(width, block_count, block_len), flat_ids, axis=1).reshape(
        width, tile_count, span
    )
    dec_sel = jnp.take(dec_weight.reshape(block_count, block_len, width), flat_ids, axis=0).reshape(
        tile_count, span, width
    )
    bias_sel = jnp.take(enc_bias.reshape(block_count, block_len), flat_ids, axis=0).reshape(
        tile_count, 1, span
    )
    level_sel = jnp.take(threshold.reshape(block_count, block_len), flat_ids, axis=0).reshape(
        tile_count, 1, span
    )
    live = (lax.broadcasted_iota(jnp.int32, (tile_count, slot_count), 1) < counts).astype(
        jnp.float32
    )
    gate_mask = jnp.repeat(live, block_len, axis=1)[:, None, :]
    enc_part = jnp.einsum("tnd,dtl->tnl", x_tiles, enc_sel, preferred_element_type=jnp.float32)
    dec_part = jnp.einsum("tnd,tld->tnl", g_tiles, dec_sel, preferred_element_type=jnp.float32)
    preact, grad_latent = lax.psum((enc_part, dec_part), "dm")
    preact = preact + bias_sel
    jump = gate_mask * jnp.clip((preact - level_sel) / band_width, 0.0, 1.0)
    active = preact * jump
    gated = grad_latent * jump
    scores = jnp.sum(active * grad_latent, axis=1)
    active_low = active.astype(jnp.bfloat16)
    gated_low = gated.astype(jnp.bfloat16)
    recon_rows = jnp.einsum(
        "tnl,tld->tnd", active_low, dec_sel, preferred_element_type=jnp.float32
    ).reshape(tile_count * tile_len, width)
    grad_rows = jnp.einsum(
        "tnl,dtl->tnd", gated_low, enc_sel, preferred_element_type=jnp.float32
    ).reshape(tile_count * tile_len, width)
    recon_part, grad_part = (
        lax.psum_scatter(recon_rows, "lat", scatter_dimension=0, tiled=True),
        lax.psum_scatter(grad_rows, "lat", scatter_dimension=0, tiled=True),
    )
    recon_full, grad_full = lax.psum((recon_part, grad_part), "sub")
    recon_out = (recon_full + dec_bias).astype(jnp.bfloat16)
    grad_out = grad_full.astype(jnp.bfloat16)
    picker = (
        flat_ids[:, None]
        == lax.broadcasted_iota(jnp.int32, (tile_count * slot_count, block_count), 1)
    ).astype(jnp.float32)
    slot_scores = scores.reshape(tile_count * slot_count, block_len)
    attribution = jnp.einsum(
        "sk,sb->kb",
        picker,
        slot_scores,
        precision=lax.Precision.HIGHEST,
        preferred_element_type=jnp.float32,
    ).reshape(block_count * block_len)
    return (recon_out, grad_out, attribution)


def solution(mesh):
    n = mesh.shape["lat"]

    def local(*args):
        tokens, blocks = args[0], args[7]
        if n == 4 and n == blocks.shape[0] and mesh.shape["dm"] == 2 and mesh.shape["sub"] == 2:
            return fused(n, *args)
        return plain(*args)

    in_specs = (
        P(("groups", "lat"), "dm"),
        P(("groups", "lat"), "dm"),
        P("dm", ("lat", "sub")),
        P(("lat", "sub")),
        P(("lat", "sub")),
        P(("lat", "sub"), "dm"),
        P("dm"),
        P("groups", ("lat", "sub"), None),
        P("groups", ("lat", "sub")),
    )
    out_specs = (
        P(("groups", "lat"), "dm"),
        P(("groups", "lat"), "dm"),
        P(("groups", "lat", "sub")),
    )
    return jax.shard_map(local, mesh=mesh, in_specs=in_specs, out_specs=out_specs, check_vma=False)
```
